256 devices in a mesh: brow: 16 (over x, y_hi, core), bcol: 16 (over y_lo, z).
Axes of the slice: x: 4, y: 4 (y_hi: 2, y_lo: 2; y = y_hi * 2 + y_lo), z: 8, core: 2. Of those that a mesh axis runs over, the one named last changes fastest.
Arguments:
- inverse_block: float32 [8192, 8192], P('brow', 'bcol'), may hold values from -8 to 8
- panels: float32 [2, 8192, 2048], P(None, 'bcol', 'brow'), may hold values from -0.06629126 to 0.06629126
- ancestor_blocks: int32 [2, 32], replicated, may hold values 0 or 1
- pattern: int32 [32, 32], P('brow', 'bcol'), may hold values 0 or 1
- diag_inverse: float32 [2, 2048, 2048], P(None, 'brow', 'bcol'), may hold values from -6 to 6
Outputs:
- sigma_ij: float32 [2, 8192, 2048], P(None, 'brow', 'bcol')
- sigma_jj: float32 [2, 2048, 2048], P(None, 'brow', 'bcol')
The draws below stay inside these ranges and needn't reach their ends.
All inputs are finite; a program needn't handle non-finite values. No bound on the sum of `pattern` on one device may be relied on, other than what follows from the above.
Results may differ from the reference program's by a relative error of at most 0.0001.
Values sent between devices are 32-bit elements; how exact they have to be, the bound alone decides.
A program may use at most 128 MiB of HBM per device.

```python
import jax
import jax.numpy as jnp
from jax import lax

W = 2048
BLOCK = 256
SNODES = 2
R = 8192
NBLK = 32


def touch_ends(drawn, rng, low, high):
    longest = drawn.shape.index(max(drawn.shape))
    spots = []
    for shift in (0, 1):
        where = [jax.random.randint(jax.random.fold_in(rng, axis), (), 0, length) for axis, length in enumerate(drawn.shape)]
        where[longest] = (where[longest] + shift) % drawn.shape[longest]
        spots.append(tuple(where))
    return drawn.at[spots[0]].set(low).at[spots[1]].set(high)


def shard_levels(key, dims, pieces, low, largest):
    factor_of, own = 1.0, jax.random.fold_in(key, 6)
    for position, parts in pieces:
        heights = jnp.exp(jax.random.uniform(jax.random.fold_in(own, position), (parts,), jnp.float32, low / len(pieces), largest / len(pieces)))
        factor_of = factor_of * jnp.repeat(heights, dims[position] // parts).reshape([-1 if axis == position else 1 for axis in range(len(dims))])
    return factor_of


def centred(own_key, shape, scale, reach, split=(), held_as=jnp.bfloat16):
    level = shard_levels(own_key, shape, split, -0.22, 0.18) if split else 1.0
    values = jax.random.normal(own_key, shape, jnp.float32) * scale * level
    return jnp.minimum(jnp.maximum(values, -reach), reach).astype(held_as)


def setup_inputs(seed: int = 0) -> dict:
    key_of = jax.random.split(jax.random.key(seed), 6)
    inverse_block = centred(key_of[0], (R, R), 1.6, 8.0, ((0, 16), (1, 16)), jnp.float32)
    panels = centred(key_of[1], (SNODES, R, W), (1.0 / (R ** 0.5)), 0.06629126, ((1, 16), (2, 16)), jnp.float32)
    ancestor_blocks = touch_ends((jax.random.randint(key_of[2], (SNODES, NBLK), 0, 5) < 4).astype(jnp.int32), jax.random.fold_in(key_of[2], 1), 0, 1)
    pattern = touch_ends((jax.random.randint(key_of[3], (NBLK, NBLK), 0, 5) < 2).astype(jnp.int32), jax.random.fold_in(key_of[3], 1), 0, 1)
    diag_inverse = centred(key_of[4], (SNODES, W, W), 1.0, 6.0, ((1, 16), (2, 16)), jnp.float32)
    return {"inverse_block": inverse_block, "panels": panels, "ancestor_blocks": ancestor_blocks, "pattern": pattern, "diag_inverse": diag_inverse}


def expand_rows(flags):
    return jnp.repeat(flags.astype(jnp.float32), BLOCK)[:, None]


def reference(inverse_block, panels, ancestor_blocks, pattern, diag_inverse):
    blocks = inverse_block.shape[0] // BLOCK
    sparse_inv = (inverse_block.reshape(blocks, BLOCK, blocks, BLOCK) * pattern.astype(jnp.float32)[:, None, :, None]).reshape(inverse_block.shape)
    outer = []
    inner = []
    for snode in range(SNODES):
        keep = expand_rows(ancestor_blocks[snode])
        panel = panels[snode] * keep
        product = jnp.dot(sparse_inv, panel, precision=lax.Precision.HIGHEST, preferred_element_type=jnp.float32)
        cross = -product * keep
        diag = diag_inverse[snode] - jnp.dot(panel.T, cross, precision=lax.Precision.HIGHEST, preferred_element_type=jnp.float32)
        outer.append(cross)
        inner.append(diag)
    return jnp.stack(outer), jnp.stack(inner)
```

```python
import functools

import jax
import jax.numpy as jnp
from jax import lax
from jax.experimental import pallas as pl
from jax.experimental.pallas import tpu as pltpu
from jax.sharding import PartitionSpec as P

MESH = pl.DeviceIdType.MESH
F32, BF16 = jnp.float32, jnp.bfloat16
BLOCK = 256
ROWS, COLS, HALF = 512, 128, 256


def split(value):
    high = value.astype(BF16)
    return high, (value - high.astype(F32)).astype(BF16)


def dot(a, b):
    return jnp.dot(a, b, preferred_element_type=F32)


def landed(ref, sem):
    pltpu.make_async_copy(ref, ref, sem).wait()


class Sends:
    def __init__(self):
        self.started = []

    def __call__(self, src, dst, send_sem, recv_sem, device):
        copy = pltpu.make_async_remote_copy(
            src_ref=src, dst_ref=dst, send_sem=send_sem, recv_sem=recv_sem, device_id=device, device_id_type=MESH
        )
        copy.start()
        self.started.append(copy)

    def finish(self):
        for copy in self.started:
            copy.wait_send()


class ReduceScatter:
    def __init__(self, send, part, slots, send_sem, recv_sem, up, down):
        self.send, self.part, self.slots = send, part, slots
        self.send_sem, self.recv_sem = send_sem, recv_sem
        self.to = (up, down)

    def hop(self, way, half, d):
        first = 4 if half == way else 3
        mine = self.part(d if way == 0 else 8 - d, half)
        if d < first:
            slot = self.slots(way, half, d)
            landed(slot, self.recv_sem.at[way, half, d])
            mine[...] = mine[...] + slot[...]
        self.send(
            mine,
            self.slots(way, half, d - 1),
            self.send_sem.at[way, half, d],
            self.recv_sem.at[way, half, d - 1],
            self.to[way],
        )

    def step(self, t):
        for way, half in ((0, 0), (1, 1), (0, 1), (1, 0)):
            first = 4 if half == way else 3
            if first - t >= 1:
                self.hop(way, half, first - t)

    def total(self, half):
        up, down = self.slots(0, half, 0), self.slots(1, half, 0)
        landed(up, self.recv_sem.at[0, half, 0])
        landed(down, self.recv_sem.at[1, half, 0])
        return self.part(0, half)[...] + up[...] + down[...]


def kernel(
    s_ref, p_ref, anc, pat, d_ref, oij, ojj,
    pm, sm, sr, sh, sl, pall, ph, pln, cp, zr, cfin, xr, ct, ot, orr, fin, fr,
    y_s, y_r, s_s, s_r, x_s, x_r, f_s, f_r, c_s, c_r, z_s, z_r, e_s, e_r, t_s, t_r, o_s, o_r, h_s, h_r,
):
    brow, bcol = lax.axis_index("brow"), lax.axis_index("bcol")
    x, yh, c = brow // 4, brow // 2 % 2, brow % 2
    yl, z = bcol // 8, bcol % 8
    y = yh * 2 + yl
    own = x * 2 + c

    def at(x, y, z, c):
        return (x * 4 + (y // 2) * 2 + c, (y % 2) * 8 + z)

    right, left = at((x + 1) % 4, y, z, c), at((x + 3) % 4, y, z, c)
    up, down = at(x, y, (z + 1) % 8, c), at(x, y, (z + 7) % 8, c)
    sibling = at(x, y, z, 1 - c)
    partner = (brow, (1 - yl) * 8 + z)
    low = brow % 8
    diagonal_t = low == z
    diagonal_h = brow == bcol
    send = Sends()

    barrier = pltpu.get_barrier_semaphore()

    def greet(device):
        pl.semaphore_signal(barrier, inc=1, device_id=device, device_id_type=MESH)

    for k in (1, 2, 3):
        greet(at(x, (y + k) % 4, z, c))
    for device in (right, left, up, down, sibling):
        greet(device)
    for k in range(2):
        pl.when(z + 8 * k != brow)(lambda k=k: greet((z + 8 * k, yl * 8 + low)))
        pl.when(jnp.logical_or(brow != bcol, brow // 8 != k))(lambda k=k: greet((bcol, k * 8 + low)))

    for half in range(2):
        rows = pl.ds(half * BLOCK, BLOCK)
        pall[own, y, rows, :] = p_ref[yl, rows, :] * anc[yl, 2 * bcol + half].astype(F32)
        pm[rows, :] = p_ref[1 - yl, rows, :] * anc[1 - yl, 2 * bcol + half].astype(F32)

    pl.semaphore_wait(
        barrier, 12 - jnp.where(diagonal_t, 1, 0) - jnp.where(diagonal_h, 1, 0)
    )

    for k in (1, 3, 2):
        send(pm if k != 2 else pall.at[own, y], pall.at[own, y], y_s.at[k], y_r.at[k], at(x, (y + k) % 4, z, c))

    def spread(r):
        piece = pall.at[own, (y + r) % 4]
        send(piece, piece, x_s.at[0, r], x_r.at[0, r], right)
        send(piece, piece, x_s.at[1, r], x_r.at[1, r], left)

    def share(column, r, k):
        piece = pall.at[column * 2 + c, (y + r) % 4]
        send(piece, piece, c_s.at[k, r], c_r.at[k, r], sibling)

    spread(0)
    share(x, 0, 0)

    for i in range(2):
        for j in range(2):
            block = (pl.ds(i * BLOCK, BLOCK), pl.ds(j * BLOCK, BLOCK))
            sm[block] = s_ref[block] * pat[i, j].astype(F32)

    for r in (1, 3, 2):
        landed(pall.at[own, (y + r) % 4], y_r.at[4 - r])
        spread(r)
        share(x, r, 0)
    for i in range(2):
        rows = pl.ds(i * BLOCK, BLOCK)
        send(sm.at[rows], sr.at[rows], s_s.at[i], s_r.at[i], partner)

    def place(ref, index):
        high, low_part = split(ref[...])
        for k in range(2):
            @pl.when(index == k)
            def _():
                sh[:, pl.ds(k * ROWS, ROWS)] = high
                sl[:, pl.ds(k * ROWS, ROWS)] = low_part

    place(sm, yl)

    before, after, across = (x + 3) % 4, (x + 1) % 4, (x + 2) % 4
    for r in (0, 1, 3, 2):
        from_left, from_right = pall.at[before * 2 + c, (y + r) % 4], pall.at[after * 2 + c, (y + r) % 4]
        landed(from_left, x_r.at[0, r])
        if r in (0, 3):
            send(from_left, from_left, f_s.at[r], f_r.at[r], right)
        share(before, r, 1)
        landed(from_right, x_r.at[1, r])
        if r in (1, 2):
            send(from_right, from_right, f_s.at[r], f_r.at[r], left)
        share(after, r, 2)

    def shared(column, r, k):
        landed(pall.at[column * 2 + 1 - c, (y + r) % 4], c_r.at[k, r])

    for i in range(2):
        rows = pl.ds(i * BLOCK, BLOCK)
        landed(sr.at[rows], s_r.at[i])
    place(sr, 1 - yl)

    def multiply(h):
        def unit(q, carry):
            u = h * 4 + q
            for k in range(4):
                high, low_part = split(pall[u, k])
                block = (u, pl.ds(k % 2 * ROWS, ROWS), pl.ds(k // 2 * COLS, COLS))
                ph[block] = high
                pln[block] = low_part
            for i in range(2):
                rows = pl.ds(i * HALF, HALF)
                a, b, value = sh[rows, :], sl[rows, :], ph[u]
                got = dot(a, pln[u]) + dot(b, value) + dot(a, value)
                for k in range(2):
                    cp[(u // 2) * 4 + k * 2 + u % 2, rows, :] = got[:, k * COLS : (k + 1) * COLS]
            return carry

        lax.fori_loop(0, 4, unit, 0)

    def reduction(h, phase):
        return ReduceScatter(
            send,
            lambda d, half: cp.at[h * 8 + (z + d) % 8, pl.ds(half * HALF, HALF)],
            lambda way, half, d: zr.at[phase, way, half, d],
            z_s.at[phase], z_r.at[phase], up, down,
        )

    def collect(reduced, h):
        for half in range(2):
            rows = pl.ds(half * HALF, HALF)
            keep = anc[yl, 2 * brow + half].astype(F32)
            cfin[h, rows, :] = reduced.total(half) * -keep
        pl.when(jnp.logical_or(jnp.logical_not(diagonal_t), brow // 8 != h))(
            lambda: pltpu.make_async_remote_copy(
                src_ref=cfin.at[h], dst_ref=ct.at[brow // 8], send_sem=t_s.at[h], recv_sem=t_r.at[brow // 8],
                device_id=(z + 8 * h, yl * 8 + low), device_id_type=MESH,
            ).start()
        )

    first = x // 2
    second = 1 - first
    for r in range(4):
        shared(x, r, 0)
        shared(before, r, 1)
        shared(after, r, 2)
    multiply(first)
    one = reduction(first, 0)
    one.step(0)
    one.step(1)
    for r in (0, 1, 3, 2):
        landed(pall.at[across * 2 + c, (y + r) % 4], f_r.at[r])
        share(across, r, 3)
    for r in range(4):
        shared(across, r, 3)
    multiply(second)
    two = reduction(second, 1)
    two.step(0)
    one.step(2)
    two.step(1)
    one.step(3)
    two.step(2)
    collect(one, first)
    two.step(3)
    collect(two, second)

    send(cfin.at[1 - yl], xr, e_s, e_r, partner)
    oij[yl] = cfin[yl]
    mine = brow // 8

    @pl.when(diagonal_t)
    def _():
        ct[mine] = cfin[mine]

    for k in range(2):
        pl.when(z + 8 * k != brow)(lambda k=k: landed(ct.at[k], t_r.at[k]))

    turned = jnp.concatenate([ct[0].T, ct[1].T], axis=1)
    high, low_part = split(turned)
    both = jnp.concatenate([high, low_part], axis=0)

    sh[pl.ds(0, 2 * COLS), :] = both

    def unit(u, carry):
        value = ph[u]
        got = dot(sh[pl.ds(0, 2 * COLS), :], value)
        got = got[:COLS] + got[COLS:] + dot(sh[pl.ds(0, COLS), :], pln[u])
        for k in range(2):
            ot[(u // 2) * 4 + k * 2 + u % 2] = got[:, k * COLS : (k + 1) * COLS]
        return carry

    lax.fori_loop(0, 8, unit, 0)
    three = ReduceScatter(
        send,
        lambda d, half: ot.at[half * 8 + (z + d) % 8],
        lambda way, half, d: orr.at[way, half, d],
        o_s, o_r, up, down,
    )
    for t in range(4):
        three.step(t)

    def home(h):
        return pltpu.make_async_remote_copy(
            src_ref=fin.at[h], dst_ref=fr.at[yl], send_sem=h_s.at[h], recv_sem=h_r.at[yl],
            device_id=(z + 8 * h, brow), device_id_type=MESH,
        )

    def away(h):
        return jnp.logical_or(jnp.logical_not(diagonal_h), yl != h)

    for h in range(2):
        fin[h] = three.total(h)
        pl.when(away(h))(lambda h=h: home(h).start())
    landed(xr, e_r)
    oij[1 - yl] = xr[...]

    @pl.when(diagonal_h)
    def _():
        fr[yl] = fin[yl]

    for k in range(2):
        pl.when(jnp.logical_or(brow != bcol, brow // 8 != k))(lambda k=k: landed(fr.at[k], h_r.at[k]))
        ojj[k] = d_ref[k] - fr[k].T

    for h in range(2):
        pl.when(away(h))(lambda h=h: home(h).wait_send())
        pl.when(jnp.logical_or(jnp.logical_not(diagonal_t), mine != h))(
            lambda h=h: pltpu.make_async_remote_copy(
                src_ref=cfin.at[h], dst_ref=ct.at[mine], send_sem=t_s.at[h], recv_sem=t_r.at[mine],
                device_id=(z + 8 * h, yl * 8 + low), device_id_type=MESH,
            ).wait_send()
        )
    send.finish()


def on_device(inverse_block, panels, ancestor_blocks, pattern, diag_inverse):
    vmem, smem = pl.BlockSpec(memory_space=pltpu.VMEM), pl.BlockSpec(memory_space=pltpu.SMEM)
    dma = pltpu.SemaphoreType.DMA
    semaphores = [(4,), (2,), (2, 4), (4,), (4, 4), (2, 2, 2, 5), (), (2,), (2, 2, 5), (2,)]
    return pl.pallas_call(
        kernel,
        out_shape=(
            jax.ShapeDtypeStruct((2, ROWS, COLS), F32),
            jax.ShapeDtypeStruct((2, COLS, COLS), F32),
        ),
        in_specs=[vmem, vmem, smem, smem, vmem],
        out_specs=(vmem, vmem),
        scratch_shapes=[
            pltpu.VMEM((ROWS, COLS), F32),
            pltpu.VMEM((ROWS, ROWS), F32),
            pltpu.VMEM((ROWS, ROWS), F32),
            pltpu.VMEM((ROWS, 2 * ROWS), BF16),
            pltpu.VMEM((ROWS, 2 * ROWS), BF16),
            pltpu.VMEM((8, 4, ROWS, COLS), F32),
            pltpu.VMEM((8, 2 * ROWS, 2 * COLS), BF16),
            pltpu.VMEM((8, 2 * ROWS, 2 * COLS), BF16),
            pltpu.VMEM((16, ROWS, COLS), F32),
            pltpu.VMEM((2, 2, 2, 4, HALF, COLS), F32),
            pltpu.VMEM((2, ROWS, COLS), F32),
            pltpu.VMEM((ROWS, COLS), F32),
            pltpu.VMEM((2, ROWS, COLS), F32),
            pltpu.VMEM((16, COLS, COLS), F32),
            pltpu.VMEM((2, 2, 4, COLS, COLS), F32),
            pltpu.VMEM((2, COLS, COLS), F32),
            pltpu.VMEM((2, COLS, COLS), F32),
        ]
        + [dma(shape) for shape in semaphores for _ in range(2)],
        compiler_params=pltpu.CompilerParams(
            collective_id=0, has_side_effects=True, vmem_limit_bytes=56 * 2**20
        ),
        cost_estimate=pl.CostEstimate(flops=8 * 10**9, bytes_accessed=3 * 2**20, transcendentals=0),
        name="selected_inverse",
    )(inverse_block, panels, ancestor_blocks, pattern, diag_inverse)


def solution(mesh):
    return jax.shard_map(
        on_device,
        mesh=mesh,
        in_specs=(
            P("brow", "bcol"),
            P(None, "bcol", "brow"),
            P(),
            P("brow", "bcol"),
            P(None, "brow", "bcol"),
        ),
        out_specs=(P(None, "brow", "bcol"), P(None, "brow", "bcol")),
        check_vma=False,
    )
```

```python
import functools

import jax
import jax.numpy as jnp
from jax import lax
from jax.experimental import pallas as pl
from jax.experimental.pallas import tpu as pltpu
from jax.sharding import PartitionSpec as P

MESH = pl.DeviceIdType.MESH
F32, BF16 = jnp.float32, jnp.bfloat16
BLOCK = 256
ROWS, COLS = 512, 128


def split(value):
    high = value.astype(BF16)
    return high, (value - high.astype(F32)).astype(BF16)


def dot(a, b):
    return jnp.dot(a, b, preferred_element_type=F32)


def landed(ref, sem):
    pltpu.make_async_copy(ref, ref, sem).wait()


class Sends:
    def __init__(self):
        self.started = []

    def __call__(self, src, dst, send_sem, recv_sem, device):
        copy = pltpu.make_async_remote_copy(
            src_ref=src, dst_ref=dst, send_sem=send_sem, recv_sem=recv_sem, device_id=device, device_id_type=MESH
        )
        copy.start()
        self.started.append(copy)

    def finish(self):
        for copy in self.started:
            copy.wait_send()


class ReduceScatter:
    def __init__(self, send, part, slots, send_sem, recv_sem, up, down):
        self.send, self.part, self.slots = send, part, slots
        self.send_sem, self.recv_sem = send_sem, recv_sem
        self.to = (up, down)

    def hop(self, way, half, d):
        first = 4 if half == way else 3
        mine = self.part(d if way == 0 else 8 - d, half)
        if d < first:
            slot = self.slots(way, half, d)
            landed(slot, self.recv_sem.at[way, half, d])
            mine[...] = mine[...] + slot[...]
        self.send(
            mine,
            self.slots(way, half, d - 1),
            self.send_sem.at[way, half, d],
            self.recv_sem.at[way, half, d - 1],
            self.to[way],
        )

    def step(self, t):
        for way, half in ((0, 0), (1, 1), (0, 1), (1, 0)):
            first = 4 if half == way else 3
            if first - t >= 1:
                self.hop(way, half, first - t)

    def total(self, half):
        up, down = self.slots(0, half, 0), self.slots(1, half, 0)
        landed(up, self.recv_sem.at[0, half, 0])
        landed(down, self.recv_sem.at[1, half, 0])
        return self.part(0, half)[...] + up[...] + down[...]


GROUPS = 2
PIECE = ROWS // 8
PART = PIECE // GROUPS
TALL = ROWS // GROUPS
UNITS = [(0, 0), (0, 3), (0, 1), (1, 0), (0, 2), (1, 3), (1, 1), (1, 2)]
PLANE = [(a, b, c) for a in (0, 3, 1, 2) for b in range(2) for c in range(2)]
LINE = [(a, b) for b in range(8) for a in range(2)][1:]


class Ring:
    def __init__(self, send, terms, slots, send_sem, recv_sem, z, to):
        self.send, self.terms, self.slots = send, terms, slots
        self.send_sem, self.recv_sem, self.z, self.to = send_sem, recv_sem, z, to

    def step(self, t):
        d = 4 - t
        for way in range(2):
            mine = self.terms.at[(self.z + (d if way == 0 else 8 - d)) % 8]
            half = pl.ds(way * (PART // 2), PART // 2)
            target = self.slots.at[way, d - 1]
            if d == 4:
                mine, target = mine.at[half], target.at[half]
            else:
                slot, into = self.slots.at[way, d], mine
                if d == 3:
                    slot, into = slot.at[half], mine.at[half]
                landed(slot, self.recv_sem.at[way, d])
                into[...] = into[...] + slot[...]
            self.send(mine, target, self.send_sem.at[way, d], self.recv_sem.at[way, d - 1], self.to[way])

    def total(self):
        for way in range(2):
            landed(self.slots.at[way, 0], self.recv_sem.at[way, 0])
        return self.terms[self.z] + self.slots[0, 0] + self.slots[1, 0]


def kernel(
    s_ref, p_ref, anc, pat, d_ref, oij, ojj,
    pm, sm, sr, sh, sl, pall, ph, pln, cp, zr, cf, cb, xo, ct, lhs, ot, orr, fin, fr,
    y_s, y_r, s_s, s_r, x_s, x_r, f_s, f_r, c_s, c_r, z_s, z_r, b_s, b_r, t_s, t_r, e_s, e_r, o_s, o_r, h_s, h_r,
):
    brow, bcol = lax.axis_index("brow"), lax.axis_index("bcol")
    x, yh, c = brow // 4, brow // 2 % 2, brow % 2
    yl, z = bcol // 8, bcol % 8
    y = yh * 2 + yl
    own = x * 2 + c
    low = brow % 8
    diagonal = brow == bcol

    def at(x, y, z, c):
        return (x * 4 + (y // 2) * 2 + c, (y % 2) * 8 + z)

    def row(a, b, c_steps):
        return (x + a) % 4 * 4 + (yh + b) % 2 * 2 + (c + c_steps) % 2

    def column(a, b):
        return (yl + a) % 2 * 8 + (z + b) % 8

    right, left = at((x + 1) % 4, y, z, c), at((x + 3) % 4, y, z, c)
    up, down = at(x, y, (z + 1) % 8, c), at(x, y, (z + 7) % 8, c)
    sibling = at(x, y, z, 1 - c)
    partner = (brow, (1 - yl) * 8 + z)
    send = Sends()

    barrier = pltpu.get_barrier_semaphore()

    def greet(device):
        pl.semaphore_signal(barrier, inc=1, device_id=device, device_id_type=MESH)

    for steps in PLANE[1:]:
        greet((row(*steps), bcol))
    for steps in LINE:
        greet((brow, column(*steps)))
    greet(at(x, (y + 3 + 2 * yl) % 4, z, c))
    for k in range(2):
        pl.when(jnp.logical_or(brow != bcol, brow // 8 != k))(lambda k=k: greet((bcol, k * 8 + low)))

    for half in range(2):
        rows = pl.ds(half * BLOCK, BLOCK)
        pall[own, y, rows, :] = p_ref[yl, rows, :] * anc[yl, 2 * bcol + half].astype(F32)
        pm[rows, :] = p_ref[1 - yl, rows, :] * anc[1 - yl, 2 * bcol + half].astype(F32)

    pl.semaphore_wait(barrier, 33 - jnp.where(diagonal, 1, 0))

    for k in (1, 3, 2):
        send(pm if k != 2 else pall.at[own, y], pall.at[own, y], y_s.at[k], y_r.at[k], at(x, (y + k) % 4, z, c))

    def spread(r):
        piece = pall.at[own, (y + r) % 4]
        send(piece, piece, x_s.at[0, r], x_r.at[0, r], right)
        send(piece, piece, x_s.at[1, r], x_r.at[1, r], left)

    def share(steps, r):
        piece = pall.at[(x + steps) % 4 * 2 + c, (y + r) % 4]
        send(piece, piece, c_s.at[steps, r], c_r.at[steps, r], sibling)

    spread(0)
    share(0, 0)

    for g in range(GROUPS):
        for p in range(8):
            for k in range(2):
                columns = pl.ds(k * BLOCK, BLOCK)
                sm[g, pl.ds(p * PART, PART), columns] = (
                    s_ref[pl.ds(p * PIECE + g * PART, PART), columns] * pat[p // 4, k].astype(F32)
                )

    def swap(g):
        send(sm.at[g], sr.at[g], s_s.at[g], s_r.at[g], partner)

    def place(g, value, index):
        high, low_part = split(value)
        for k in range(2):
            @pl.when(index == k)
            def _():
                sh[g, :, pl.ds(k * ROWS, ROWS)] = high
                sl[g, :, pl.ds(k * ROWS, ROWS)] = low_part

    for r in (1, 3, 2):
        landed(pall.at[own, (y + r) % 4], y_r.at[4 - r])
        spread(r)
        share(0, r)
    for g in range(GROUPS):
        swap(g)
    for g in range(GROUPS):
        place(g, sm[g], yl)

    def neighbours(r):
        from_left, from_right = pall.at[(x + 3) % 4 * 2 + c, (y + r) % 4], pall.at[(x + 1) % 4 * 2 + c, (y + r) % 4]
        landed(from_left, x_r.at[0, r])
        if r in (0, 3):
            send(from_left, from_left, f_s.at[r], f_r.at[r], right)
        share(3, r)
        landed(from_right, x_r.at[1, r])
        if r in (1, 2):
            send(from_right, from_right, f_s.at[r], f_r.at[r], left)
        share(1, r)

    def opposite(r):
        landed(pall.at[(x + 2) % 4 * 2 + c, (y + r) % 4], f_r.at[r])
        share(2, r)

    def swapped(g):
        landed(sr.at[g], s_r.at[g])
        place(g, sr[g], 1 - yl)

    def prepare(steps):
        for r in range(4):
            landed(pall.at[(x + steps) % 4 * 2 + 1 - c, (y + r) % 4], c_r.at[steps, r])

        def one(q, carry):
            u = (x + steps) % 4 * 2 + q
            for k in range(4):
                high, low_part = split(pall[u, k])
                block = (u, pl.ds(k % 2 * ROWS, ROWS), pl.ds(k // 2 * COLS, COLS))
                ph[block] = high
                pln[block] = low_part
            return carry

        lax.fori_loop(0, 2, one, 0)

    def multiply(n):
        g, steps = UNITS[n]
        for q in range(2):
            u = (x + steps) % 4 * 2 + q
            a, b, value = sh[g], sl[g], ph[u]
            got = dot(a, pln[u]) + dot(b, value) + dot(a, value)
            cp[n, :, :, pl.ds(q * 2 * COLS, 2 * COLS)] = got.reshape(8, PART, 2 * COLS)

    rings = [
        Ring(send, cp.at[n], zr.at[n], z_s.at[n], z_r.at[n], z, (up, down)) for n in range(len(UNITS))
    ]
    keep = -anc[yl, 2 * brow + z // 4].astype(F32)

    def finish(n):
        g, steps = UNITS[n]
        total = rings[n].total() * keep
        for q in range(2):
            for k in range(2):
                j = (x + steps) % 4 * 4 + k * 2 + q
                block = q * 2 + k
                cf[j, pl.ds(g * PART, PART), :] = total[:, block * COLS : (block + 1) * COLS]
        if g == GROUPS - 1:
            for index, (a, b, d) in enumerate(PLANE):
                if a == steps and index:
                    j = row(a, b, d)
                    send(cf.at[j], cb.at[brow], b_s.at[index], b_r.at[index], (j, bcol))

    def onward(index, i):
        return pltpu.make_async_remote_copy(
            src_ref=cb.at[i], dst_ref=ct.at[i // 8, z], send_sem=t_s.at[index // 8, index % 8], recv_sem=t_r.at[i // 8, z],
            device_id=(brow, yl * 8 + i % 8), device_id_type=MESH,
        )

    def relay(steps):
        for index, (a, b, d) in enumerate(PLANE):
            if a != steps:
                continue
            i = (x + 4 - a) % 4 * 4 + (yh + b) % 2 * 2 + (c + d) % 2
            if index:
                landed(cb.at[i], b_r.at[index])
            else:
                cb[i] = cf[i]

            @pl.when(i % 8 == z)
            def _():
                ct[i // 8, z] = cb[i]

            pl.when(i % 8 != z)(lambda: onward(index, i).start())

    neighbours(0)
    neighbours(1)
    for time in range(len(UNITS) + 4):
        if time == 0:
            swapped(0)
            prepare(0)
        if time == 1:
            neighbours(3)
            neighbours(2)
            prepare(3)
        if time == 2:
            prepare(1)
        if time == 3:
            swapped(1)
        if time == 4:
            for r in (0, 1, 3, 2):
                opposite(r)
            prepare(2)
        if time < len(UNITS):
            multiply(time)
            rings[time].step(0)
        for t in (3, 2, 1):
            if 0 <= time - t < len(UNITS):
                rings[time - t].step(t)
        if time >= 4:
            finish(time - 4)
        if time == 9:
            relay(0)
        if time == 10:
            relay(3)
    relay(1)
    relay(2)

    for k in range(2):
        for d in range(1, 8):
            landed(ct.at[k, (z + d) % 8], t_r.at[k, (z + d) % 8])
    for index, (a, b) in enumerate(LINE):
        send(cf.at[column(a, b)], xo.at[yl, z], e_s.at[index], e_r.at[index], (brow, column(a, b)))
    xo[yl, z] = cf[bcol]

    turned = jnp.concatenate([ct[k].reshape(ROWS, COLS).T for k in range(2)], axis=1)
    high, low_part = split(turned)
    lhs[pl.ds(0, COLS), :] = high
    lhs[pl.ds(COLS, COLS), :] = low_part

    def unit(u, carry):
        got = dot(lhs[...], ph[u])
        got = got[:COLS] + got[COLS:] + dot(lhs[pl.ds(0, COLS), :], pln[u])
        for k in range(2):
            ot[(u // 2) * 4 + k * 2 + u % 2] = got[:, k * COLS : (k + 1) * COLS]
        return carry

    lax.fori_loop(0, 8, unit, 0)
    last = ReduceScatter(
        send,
        lambda d, half: ot.at[half * 8 + (z + d) % 8],
        lambda way, half, d: orr.at[way, half, d],
        o_s, o_r, up, down,
    )
    for t in range(4):
        last.step(t)

    def home(h):
        return pltpu.make_async_remote_copy(
            src_ref=fin.at[h], dst_ref=fr.at[yl], send_sem=h_s.at[h], recv_sem=h_r.at[yl],
            device_id=(z + 8 * h, brow), device_id_type=MESH,
        )

    def away(h):
        return jnp.logical_or(jnp.logical_not(diagonal), yl != h)

    for h in range(2):
        fin[h] = last.total(h)
        pl.when(away(h))(lambda h=h: home(h).start())
    for index, (a, b) in enumerate(LINE):
        landed(xo.at[(yl + a) % 2, (z + 8 - b) % 8], e_r.at[index])
    oij[...] = xo[...].reshape(2, ROWS, COLS)

    @pl.when(diagonal)
    def _():
        fr[yl] = fin[yl]

    for k in range(2):
        pl.when(jnp.logical_or(brow != bcol, brow // 8 != k))(lambda k=k: landed(fr.at[k], h_r.at[k]))
        ojj[k] = d_ref[k] - fr[k].T

    for h in range(2):
        pl.when(away(h))(lambda h=h: home(h).wait_send())
    for index, (a, b, d) in enumerate(PLANE):
        i = (x + 4 - a) % 4 * 4 + (yh + b) % 2 * 2 + (c + d) % 2
        pl.when(i % 8 != z)(lambda: onward(index, i).wait_send())
    send.finish()


def on_device(inverse_block, panels, ancestor_blocks, pattern, diag_inverse):
    vmem, smem = pl.BlockSpec(memory_space=pltpu.VMEM), pl.BlockSpec(memory_space=pltpu.SMEM)
    dma = pltpu.SemaphoreType.DMA
    count = len(UNITS)
    semaphores = [
        (4,), (GROUPS,), (2, 4), (4,), (4, 4), (count, 2, 5), (16,), (2, 8), (15,), (2, 2, 5), (2,)
    ]
    return pl.pallas_call(
        kernel,
        out_shape=(
            jax.ShapeDtypeStruct((2, ROWS, COLS), F32),
            jax.ShapeDtypeStruct((2, COLS, COLS), F32),
        ),
        in_specs=[vmem, vmem, smem, smem, vmem],
        out_specs=(vmem, vmem),
        scratch_shapes=[
            pltpu.VMEM((ROWS, COLS), F32),
            pltpu.VMEM((GROUPS, TALL, ROWS), F32),
            pltpu.VMEM((GROUPS, TALL, ROWS), F32),
            pltpu.VMEM((GROUPS, TALL, 2 * ROWS), BF16),
            pltpu.VMEM((GROUPS, TALL, 2 * ROWS), BF16),
            pltpu.VMEM((8, 4, ROWS, COLS), F32),
            pltpu.VMEM((8, 2 * ROWS, 2 * COLS), BF16),
            pltpu.VMEM((8, 2 * ROWS, 2 * COLS), BF16),
            pltpu.VMEM((count, 8, PART, 4 * COLS), F32),
            pltpu.VMEM((count, 2, 4, PART, 4 * COLS), F32),
            pltpu.VMEM((16, PIECE, COLS), F32),
            pltpu.VMEM((16, PIECE, COLS), F32),
            pltpu.VMEM((2, 8, PIECE, COLS), F32),
            pltpu.VMEM((2, 8, PIECE, COLS), F32),
            pltpu.VMEM((2 * COLS, 2 * ROWS), BF16),
            pltpu.VMEM((16, COLS, COLS), F32),
            pltpu.VMEM((2, 2, 4, COLS, COLS), F32),
            pltpu.VMEM((2, COLS, COLS), F32),
            pltpu.VMEM((2, COLS, COLS), F32),
        ]
        + [dma(shape) for shape in semaphores for _ in range(2)],
        compiler_params=pltpu.CompilerParams(
            collective_id=0, has_side_effects=True, vmem_limit_bytes=56 * 2**20
        ),
        cost_estimate=pl.CostEstimate(flops=8 * 10**9, bytes_accessed=3 * 2**20, transcendentals=0),
        name="selected_inverse",
    )(inverse_block, panels, ancestor_blocks, pattern, diag_inverse)


def solution(mesh):
    return jax.shard_map(
        on_device,
        mesh=mesh,
        in_specs=(
            P("brow", "bcol"),
            P(None, "bcol", "brow"),
            P(),
            P("brow", "bcol"),
            P(None, "brow", "bcol"),
        ),
        out_specs=(P(None, "brow", "bcol"), P(None, "brow", "bcol")),
        check_vma=False,
    )
```

```python
import functools

import jax
import jax.numpy as jnp
from jax import lax
from jax.experimental import pallas as pl
from jax.experimental.pallas import tpu as pltpu
from jax.sharding import PartitionSpec as P

MESH = pl.DeviceIdType.MESH
F32, BF16 = jnp.float32, jnp.bfloat16
BLOCK = 256
ROWS, COLS = 512, 128


def split(value):
    high = value.astype(BF16)
    return high, (value - high.astype(F32)).astype(BF16)


def dot(a, b):
    return jnp.dot(a, b, preferred_element_type=F32)


def landed(ref, sem):
    pltpu.make_async_copy(ref, ref, sem).wait()


class Sends:
    def __init__(self):
        self.started, self.done = [], 0

    def __call__(self, src, dst, send_sem, recv_sem, device):
        copy = pltpu.make_async_remote_copy(
            src_ref=src, dst_ref=dst, send_sem=send_sem, recv_sem=recv_sem, device_id=device, device_id_type=MESH
        )
        copy.start()
        self.started.append(copy)

    def finish(self, upto=None):
        upto = len(self.started) if upto is None else upto
        while self.done < upto:
            self.started[self.done].wait_send()
            self.done += 1


class ReduceScatter:
    def __init__(self, send, part, slots, send_sem, recv_sem, up, down):
        self.send, self.part, self.slots = send, part, slots
        self.send_sem, self.recv_sem = send_sem, recv_sem
        self.to = (up, down)

    def hop(self, way, half, d):
        first = 4 if half == way else 3
        mine = self.part(d if way == 0 else 8 - d, half)
        if d < first:
            slot = self.slots(way, half, d)
            landed(slot, self.recv_sem.at[way, half, d])
            mine[...] = mine[...] + slot[...]
        self.send(
            mine,
            self.slots(way, half, d - 1),
            self.send_sem.at[way, half, d],
            self.recv_sem.at[way, half, d - 1],
            self.to[way],
        )

    def step(self, t):
        for way, half in ((0, 0), (1, 1), (0, 1), (1, 0)):
            first = 4 if half == way else 3
            if first - t >= 1:
                self.hop(way, half, first - t)

    def total(self, half):
        up, down = self.slots(0, half, 0), self.slots(1, half, 0)
        landed(up, self.recv_sem.at[0, half, 0])
        landed(down, self.recv_sem.at[1, half, 0])
        return self.part(0, half)[...] + up[...] + down[...]


GROUPS = 2
PIECE = ROWS // 8
PART = PIECE // GROUPS
TALL = ROWS // GROUPS
LAG = 2
UNITS = [
    (0, 0, 0), (0, 3, 0), (0, 1, 0), (0, 2, 0), (0, 0, 1), (0, 3, 1), (0, 1, 1), (1, 0, 0),
    (1, 3, 0), (1, 1, 0), (1, 2, 0), (1, 0, 1), (0, 2, 1), (1, 3, 1), (1, 1, 1), (1, 2, 1),
]
PLANE = [(a, b, c) for b in range(2) for a in (0, 3, 1, 2) for c in range(2)]
LINE = [(a, b) for b in range(8) for a in range(2)][1:]


class Ring:
    def __init__(self, send, terms, slots, send_sem, recv_sem, z, to):
        self.send, self.terms, self.slots = send, terms, slots
        self.send_sem, self.recv_sem, self.z, self.to = send_sem, recv_sem, z, to

    def step(self, t):
        d = 4 - t
        for way in range(2):
            mine = self.terms.at[(self.z + (d if way == 0 else 8 - d)) % 8]
            half = pl.ds(way * (PART // 2), PART // 2)
            target = self.slots.at[way, d - 1]
            if d == 4:
                mine, target = mine.at[half], target.at[half]
            else:
                slot, into = self.slots.at[way, d], mine
                if d == 3:
                    slot, into = slot.at[half], mine.at[half]
                landed(slot, self.recv_sem.at[way, d])
                into[...] = into[...] + slot[...]
            self.send(mine, target, self.send_sem.at[way, d], self.recv_sem.at[way, d - 1], self.to[way])

    def total(self):
        for way in range(2):
            landed(self.slots.at[way, 0], self.recv_sem.at[way, 0])
        return self.terms[self.z] + self.slots[0, 0] + self.slots[1, 0]


class Gather:
    def __init__(self, send, buf, high, low_part, place, devices, x_s, x_r, f_s, f_r, c_s, c_r):
        self.send, self.buf, self.high, self.low_part = send, buf, high, low_part
        self.x, self.yh, self.yl, self.c = place
        self.right, self.left, self.sibling = devices
        self.x_s, self.x_r, self.f_s, self.f_r, self.c_s, self.c_r = x_s, x_r, f_s, f_r, c_s, c_r

    def piece(self, steps, r, other=0):
        y = (self.yh + r // 2) % 2 * 2 + (self.yl + r % 2) % 2
        return self.buf.at[(self.x + steps) % 4 * 2 + (self.c + other) % 2, y]

    def spread(self, r):
        piece = self.piece(0, r)
        self.send(piece, piece, self.x_s.at[0, r], self.x_r.at[0, r], self.right)
        self.send(piece, piece, self.x_s.at[1, r], self.x_r.at[1, r], self.left)
        self.share(0, r)

    def share(self, steps, r):
        piece = self.piece(steps, r)
        self.send(piece, piece, self.c_s.at[steps, r], self.c_r.at[steps, r], self.sibling)

    def neighbours(self, r):
        for side, steps, onward, forward in ((0, 3, self.right, (0, 3)), (1, 1, self.left, (1, 2))):
            piece = self.piece(steps, r)
            landed(piece, self.x_r.at[side, r])
            if r in forward:
                self.send(piece, piece, self.f_s.at[r], self.f_r.at[r], onward)
            self.share(steps, r)

    def opposite(self, r):
        landed(self.piece(2, r), self.f_r.at[r])
        self.share(2, r)

    def prepare(self, steps, turn):
        a, b = (self.x + steps) % 4, (self.yh + turn) % 2
        for r in (2 * turn, 2 * turn + 1):
            landed(self.piece(steps, r, 1), self.c_r.at[steps, r])
        for q in range(2):
            for k in range(2):
                high, low_part = split(self.buf[a * 2 + q, b * 2 + k])
                block = (a * 2 + b, pl.ds(k * ROWS, ROWS), pl.ds(q * COLS, COLS))
                self.high[block] = high
                self.low_part[block] = low_part


def kernel(
    s_ref, p_ref, anc, pat, d_ref, oij, ojj,
    pm, sm, sr, sh, sl, pall, ph, pln, pq, pall2, ph2, pln2, cp, zr, cf, cb, xo, lhs, ot, orr, fin, fr,
    y_s, y_r, s_s, s_r, x_s, x_r, f_s, f_r, c_s, c_r, z_s, z_r, b_s, b_r, e_s, e_r, o_s, o_r, h_s, h_r,
    q_s, q_r, y2_s, y2_r, x2_s, x2_r, f2_s, f2_r, c2_s, c2_r,
):
    brow, bcol = lax.axis_index("brow"), lax.axis_index("bcol")
    x, yh, c = brow // 4, brow // 2 % 2, brow % 2
    yl, z = bcol // 8, bcol % 8
    y = yh * 2 + yl
    own = x * 2 + c
    low = brow % 8
    diagonal = brow == bcol

    def at(x, y, z, c):
        return (x * 4 + (y // 2) * 2 + c, (y % 2) * 8 + z)

    def across_y(r):
        return (yh + r // 2) % 2 * 2 + (yl + r % 2) % 2

    def row(a, b, c_steps):
        return (x + a) % 4 * 4 + (yh + b) % 2 * 2 + (c + c_steps) % 2

    def column(a, b):
        return (yl + a) % 2 * 8 + (z + b) % 8

    right, left = at((x + 1) % 4, y, z, c), at((x + 3) % 4, y, z, c)
    up, down = at(x, y, (z + 1) % 8, c), at(x, y, (z + 7) % 8, c)
    sibling = at(x, y, z, 1 - c)
    partner = (brow, (1 - yl) * 8 + z)
    send = Sends()

    barrier = pltpu.get_barrier_semaphore()

    def greet(device):
        pl.semaphore_signal(barrier, inc=1, device_id=device, device_id_type=MESH)

    for steps in PLANE[1:]:
        greet((row(*steps), bcol))
    for steps in LINE:
        greet((brow, column(*steps)))
    greet(at(x, across_y(3), z, c))
    for k in range(2):
        pl.when(jnp.logical_or(brow != bcol, brow // 8 != k))(lambda k=k: greet((bcol, k * 8 + low)))

    for half in range(2):
        rows = pl.ds(half * BLOCK, BLOCK)
        pall[own, y, rows, :] = p_ref[yl, rows, :] * anc[yl, 2 * bcol + half].astype(F32)
        pm[rows, :] = p_ref[1 - yl, rows, :] * anc[1 - yl, 2 * bcol + half].astype(F32)

    pl.semaphore_wait(barrier, 33 - jnp.where(diagonal, 1, 0))

    def to_y(r):
        source = pm if r % 2 else pall.at[own, y]
        send(source, pall.at[own, y], y_s.at[r], y_r.at[r], at(x, across_y(r), z, c))

    devices = (right, left, sibling)
    one = Gather(send, pall, ph, pln, (x, yh, yl, c), devices, x_s, x_r, f_s, f_r, c_s, c_r)
    two = Gather(send, pall2, ph2, pln2, (x, yh, yl, c), devices, x2_s, x2_r, f2_s, f2_r, c2_s, c2_r)

    def from_y(r):
        landed(pall.at[own, across_y(r)], y_r.at[r])
        one.spread(r)

    def rows_of(step):
        return pl.ds(pl.multiple_of((z + step) % 8 * PIECE, PIECE), PIECE)

    def scatter():
        for step in range(1, 8):
            device = (brow, yl * 8 + (z + step) % 8)
            send(pall.at[own, y, rows_of(step)], pall2.at[own, y, rows_of(0)], q_s.at[0, step], q_r.at[0, step], device)
            send(pm.at[rows_of(step)], pq.at[rows_of(0)], q_s.at[1, step], q_r.at[1, step], device)
        pall2[own, y, rows_of(0), :] = pall[own, y, rows_of(0), :]
        pq[rows_of(0), :] = pm[rows_of(0), :]

    def scattered():
        for step in range(1, 8):
            landed(pall2.at[own, y, rows_of(8 - step)], q_r.at[0, step])
            landed(pq.at[rows_of(8 - step)], q_r.at[1, step])

    def to_y2(r):
        source = pq if r == 1 else pall2.at[own, across_y(r - 2)]
        target = y if r == 1 else across_y(r - 2)
        send(source, pall2.at[own, target], y2_s.at[r], y2_r.at[r], at(x, across_y(1 if r == 1 else 2), z, c))

    def from_y2(r):
        landed(pall2.at[own, across_y(r)], y2_r.at[r])
        two.spread(r)

    def swap(g):
        send(sm.at[g], sr.at[g], s_s.at[g], s_r.at[g], partner)

    to_y(1)
    to_y(3)
    one.spread(0)
    scatter()

    for g in range(GROUPS):
        for p in range(8):
            for k in range(2):
                columns = pl.ds(k * BLOCK, BLOCK)
                sm[g, pl.ds(p * PART, PART), columns] = (
                    s_ref[pl.ds(p * PIECE + g * PART, PART), columns] * pat[p // 4, k].astype(F32)
                )

    def place(g, value, index):
        high, low_part = split(value)
        for k in range(2):
            @pl.when(index == k)
            def _():
                sh[g, :, pl.ds(k * ROWS, ROWS)] = high
                sl[g, :, pl.ds(k * ROWS, ROWS)] = low_part

    def swapped(g):
        landed(sr.at[g], s_r.at[g])
        place(g, sr[g], 1 - yl)

    def multiply(n):
        g, steps, turn = UNITS[n]
        v = (x + steps) % 4 * 2 + (yh + turn) % 2
        a, b, value = sh[g], sl[g], ph[v]
        got = dot(a, pln[v]) + dot(b, value) + dot(a, value)
        cp[n] = got.reshape(8, PART, 2 * COLS)

    rings = [
        Ring(send, cp.at[n], zr.at[n], z_s.at[n], z_r.at[n], z, (up, down)) for n in range(len(UNITS))
    ]
    keep = -anc[yl, 2 * brow + z // 4].astype(F32)

    def finish(n):
        g, steps, turn = UNITS[n]
        total = rings[n].total() * keep
        for q in range(2):
            j = (x + steps) % 4 * 4 + (yh + turn) % 2 * 2 + q
            cf[j, pl.ds(g * PART, PART), :] = total[:, q * COLS : (q + 1) * COLS]
        if g == GROUPS - 1:
            for index, (a, b, d) in enumerate(PLANE):
                if (a, b) == (steps, turn) and index:
                    j = row(a, b, d)
                    send(cf.at[j], cb.at[brow], b_s.at[index], b_r.at[index], (j, bcol))

    def source(a, b, d):
        return row((4 - a) % 4, b, d)

    def out(first, last):
        for index in range(first, min(last, len(LINE))):
            a, b = LINE[index]
            send(cf.at[column(a, b)], xo.at[yl, z], e_s.at[index], e_r.at[index], (brow, column(a, b)))

    for g in range(GROUPS):
        place(g, sm[g], yl)
    from_y(1)
    swap(0)
    one.neighbours(0)
    from_y(3)
    one.neighbours(1)
    marks = []
    for time in range(len(UNITS) + 4 * LAG):
        for t in (3, 2, 1):
            if 0 <= time - t * LAG < len(UNITS):
                rings[time - t * LAG].step(t)
        if time == 0:
            swapped(0)
            to_y(2)
        if time == 1:
            scattered()
        if time == 3:
            from_y(2)
            swap(1)
            one.opposite(0)
            one.opposite(1)
        if time == 4:
            one.neighbours(3)
            two.spread(0)
        if time == 5:
            one.neighbours(2)
        if time == 7:
            swapped(1)
            to_y2(1)
            to_y2(2)
        if time == 9:
            two.neighbours(0)
        if time == 10:
            from_y2(1)
            to_y2(3)
        if time == 12:
            one.opposite(3)
            one.opposite(2)
            from_y2(2)
        if time == 14:
            two.prepare(0, 0)
            from_y2(3)
        if time == 16:
            two.neighbours(1)
            two.prepare(3, 0)
            two.prepare(1, 0)
        if time == 18:
            two.neighbours(2)
            two.prepare(0, 1)
        if time == 21:
            two.neighbours(3)
        if time == 22:
            two.prepare(3, 1)
        if time == 23:
            two.prepare(1, 1)
        if time < len(UNITS):
            g, steps, turn = UNITS[time]
            if g == 0:
                one.prepare(steps, turn)
            multiply(time)
            rings[time].step(0)
        if time >= 4 * LAG:
            finish(time - 4 * LAG)
        marks.append(len(send.started))
        if time >= 8:
            send.finish(marks[time - 8])
    cb[brow] = cf[brow]
    out(0, 15)
    for r in range(4):
        two.opposite(r)
    for index, steps in enumerate(PLANE[1:], 1):
        landed(cb.at[source(*steps)], b_r.at[index])

    turned = jnp.concatenate([cb[pl.ds(k * 8, 8)].reshape(ROWS, COLS).T for k in range(2)], axis=1)
    high, low_part = split(turned)
    lhs[pl.ds(0, COLS), :] = high
    lhs[pl.ds(COLS, COLS), :] = low_part

    def unit(v, carry):
        value = ph2[v]
        got = dot(lhs[...], value)
        got = got[:COLS] + got[COLS:] + dot(lhs[pl.ds(0, COLS), :], pln2[v])
        for q in range(2):
            ot[v * 2 + q] = got[:, q * COLS : (q + 1) * COLS]
        return carry

    two.prepare(2, 0)
    two.prepare(2, 1)
    lax.fori_loop(0, 8, unit, 0)
    last = ReduceScatter(
        send,
        lambda d, half: ot.at[half * 8 + (z + d) % 8],
        lambda way, half, d: orr.at[way, half, d],
        o_s, o_r, up, down,
    )
    for t in range(4):
        last.step(t)
        if t == 0:
            send.finish(marks[-4])
    xo[yl, z] = cf[bcol]

    def home(h):
        return pltpu.make_async_remote_copy(
            src_ref=fin.at[h], dst_ref=fr.at[yl], send_sem=h_s.at[h], recv_sem=h_r.at[yl],
            device_id=(z + 8 * h, brow), device_id_type=MESH,
        )

    def away(h):
        return jnp.logical_or(jnp.logical_not(diagonal), yl != h)

    for h in range(2):
        fin[h] = last.total(h)
        pl.when(away(h))(lambda h=h: home(h).start())
    for index, (a, b) in enumerate(LINE):
        landed(xo.at[(yl + a) % 2, (z + 8 - b) % 8], e_r.at[index])
    oij[...] = xo[...].reshape(2, ROWS, COLS)

    @pl.when(diagonal)
    def _():
        fr[yl] = fin[yl]

    for k in range(2):
        pl.when(jnp.logical_or(brow != bcol, brow // 8 != k))(lambda k=k: landed(fr.at[k], h_r.at[k]))
        ojj[k] = d_ref[k] - fr[k].T

    for h in range(2):
        pl.when(away(h))(lambda h=h: home(h).wait_send())
    send.finish()


def on_device(inverse_block, panels, ancestor_blocks, pattern, diag_inverse):
    vmem, smem = pl.BlockSpec(memory_space=pltpu.VMEM), pl.BlockSpec(memory_space=pltpu.SMEM)
    dma = pltpu.SemaphoreType.DMA
    count = len(UNITS)
    semaphores = [
        (4,), (GROUPS,), (2, 4), (4,), (4, 4), (count, 2, 5), (16,), (15,), (2, 2, 5), (2,), (2, 8), (4,), (2, 4), (4,), (4, 4)
    ]
    return pl.pallas_call(
        kernel,
        out_shape=(
            jax.ShapeDtypeStruct((2, ROWS, COLS), F32),
            jax.ShapeDtypeStruct((2, COLS, COLS), F32),
        ),
        in_specs=[vmem, vmem, smem, smem, vmem],
        out_specs=(vmem, vmem),
        scratch_shapes=[
            pltpu.VMEM((ROWS, COLS), F32),
            pltpu.VMEM((GROUPS, TALL, ROWS), F32),
            pltpu.VMEM((GROUPS, TALL, ROWS), F32),
            pltpu.VMEM((GROUPS, TALL, 2 * ROWS), BF16),
            pltpu.VMEM((GROUPS, TALL, 2 * ROWS), BF16),
            pltpu.VMEM((8, 4, ROWS, COLS), F32),
            pltpu.VMEM((8, 2 * ROWS, 2 * COLS), BF16),
            pltpu.VMEM((8, 2 * ROWS, 2 * COLS), BF16),
            pltpu.VMEM((ROWS, COLS), F32),
            pltpu.VMEM((8, 4, ROWS, COLS), F32),
            pltpu.VMEM((8, 2 * ROWS, 2 * COLS), BF16),
            pltpu.VMEM((8, 2 * ROWS, 2 * COLS), BF16),
            pltpu.VMEM((count, 8, PART, 2 * COLS), F32),
            pltpu.VMEM((count, 2, 4, PART, 2 * COLS), F32),
            pltpu.VMEM((16, PIECE, COLS), F32),
            pltpu.VMEM((16, PIECE, COLS), F32),
            pltpu.VMEM((2, 8, PIECE, COLS), F32),
            pltpu.VMEM((2 * COLS, 2 * ROWS), BF16),
            pltpu.VMEM((16, COLS, COLS), F32),
            pltpu.VMEM((2, 2, 4, COLS, COLS), F32),
            pltpu.VMEM((2, COLS, COLS), F32),
            pltpu.VMEM((2, COLS, COLS), F32),
        ]
        + [dma(shape) for shape in semaphores for _ in range(2)],
        compiler_params=pltpu.CompilerParams(
            collective_id=0, has_side_effects=True, vmem_limit_bytes=60 * 2**20
        ),
        cost_estimate=pl.CostEstimate(flops=8 * 10**9, bytes_accessed=3 * 2**20, transcendentals=0),
        name="selected_inverse",
    )(inverse_block, panels, ancestor_blocks, pattern, diag_inverse)


def solution(mesh):
    return jax.shard_map(
        on_device,
        mesh=mesh,
        in_specs=(
            P("brow", "bcol"),
            P(None, "bcol", "brow"),
            P(),
            P("brow", "bcol"),
            P(None, "brow", "bcol"),
        ),
        out_specs=(P(None, "brow", "bcol"), P(None, "brow", "bcol")),
        check_vma=False,
    )
```

```python
import functools

import jax
import jax.numpy as jnp
from jax import lax
from jax.experimental import pallas as pl
from jax.experimental.pallas import tpu as pltpu
from jax.sharding import PartitionSpec as P

MESH = pl.DeviceIdType.MESH
F32, BF16 = jnp.float32, jnp.bfloat16
BLOCK = 256
ROWS, COLS = 512, 128


def split(value):
    high = value.astype(BF16)
    return high, (value - high.astype(F32)).astype(BF16)


def dot(a, b):
    return jnp.dot(a, b, preferred_element_type=F32)


def landed(ref, sem):
    pltpu.make_async_copy(ref, ref, sem).wait()


def send(src, dst, send_sem, recv_sem, device):
    pltpu.make_async_remote_copy(
        src_ref=src, dst_ref=dst, send_sem=send_sem, recv_sem=recv_sem, device_id=device, device_id_type=MESH
    ).start()


class ReduceScatter:
    def __init__(self, part, slots, send_sem, recv_sem, up, down):
        self.part, self.slots = part, slots
        self.send_sem, self.recv_sem = send_sem, recv_sem
        self.to = (up, down)

    def hop(self, way, half, d):
        first = 4 if half == way else 3
        mine = self.part(d if way == 0 else 8 - d, half)
        if d < first:
            slot = self.slots(way, half, d)
            landed(slot, self.recv_sem.at[way, half, d])
            mine[...] = mine[...] + slot[...]
        send(
            mine,
            self.slots(way, half, d - 1),
            self.send_sem,
            self.recv_sem.at[way, half, d - 1],
            self.to[way],
        )

    def step(self, t):
        for way, half in ((0, 0), (1, 1), (0, 1), (1, 0)):
            first = 4 if half == way else 3
            if first - t >= 1:
                self.hop(way, half, first - t)

    def total(self, half):
        up, down = self.slots(0, half, 0), self.slots(1, half, 0)
        landed(up, self.recv_sem.at[0, half, 0])
        landed(down, self.recv_sem.at[1, half, 0])
        return self.part(0, half)[...] + up[...] + down[...]


GROUPS = 2
PIECE = ROWS // 8
PART = PIECE // GROUPS
TALL = ROWS // GROUPS
LAG = 2
UNITS = [
    (0, 0, 0), (0, 3, 0), (0, 1, 0), (0, 2, 0), (0, 0, 1), (0, 3, 1), (0, 1, 1), (1, 0, 0),
    (1, 3, 0), (1, 1, 0), (1, 2, 0), (1, 0, 1), (0, 2, 1), (1, 3, 1), (1, 1, 1), (1, 2, 1),
]
PLANE = [(a, b, c) for b in range(2) for a in (0, 3, 1, 2) for c in range(2)]
LINE = [(a, b) for b in range(8) for a in range(2)][1:]


class Ring:
    def __init__(self, terms, slots, send_sem, recv_sem, z, to):
        self.terms, self.slots = terms, slots
        self.send_sem, self.recv_sem, self.z, self.to = send_sem, recv_sem, z, to

    def step(self, t):
        d = 4 - t
        for way in range(2):
            mine = self.terms.at[(self.z + (d if way == 0 else 8 - d)) % 8]
            half = pl.ds(way * (PART // 2), PART // 2)
            target = self.slots.at[way, d - 1]
            if d == 4:
                mine, target = mine.at[half], target.at[half]
            else:
                slot, into = self.slots.at[way, d], mine
                if d == 3:
                    slot, into = slot.at[half], mine.at[half]
                landed(slot, self.recv_sem.at[way, d])
                into[...] = into[...] + slot[...]
            send(mine, target, self.send_sem, self.recv_sem.at[way, d - 1], self.to[way])

    def total(self):
        for way in range(2):
            landed(self.slots.at[way, 0], self.recv_sem.at[way, 0])
        return self.terms[self.z] + self.slots[0, 0] + self.slots[1, 0]


class Gather:
    def __init__(self, buf, high, low_part, turns, place, devices, x_s, x_r, f_s, f_r, c_s, c_r):
        self.buf, self.high, self.low_part, self.turns = buf, high, low_part, turns
        self.x, self.yh, self.yl, self.c = place
        self.right, self.left, self.sibling = devices
        self.x_s, self.x_r, self.f_s, self.f_r, self.c_s, self.c_r = x_s, x_r, f_s, f_r, c_s, c_r

    def piece(self, steps, r, other=0):
        block = (self.yh + r // 2) % self.turns * 2 + (self.yl + r % 2) % 2
        return self.buf.at[(self.x + steps) % 4 * 2 + (self.c + other) % 2, block]

    def spread(self, r):
        piece = self.piece(0, r)
        send(piece, piece, self.x_s, self.x_r.at[0, r], self.right)
        send(piece, piece, self.x_s, self.x_r.at[1, r], self.left)
        self.share(0, r)

    def share(self, steps, r):
        piece = self.piece(steps, r)
        send(piece, piece, self.c_s, self.c_r.at[steps, r // 2], self.sibling)

    def neighbours(self, r):
        for side, steps, onward, forward in ((0, 3, self.right, (0, 3)), (1, 1, self.left, (1, 2))):
            piece = self.piece(steps, r)
            landed(piece, self.x_r.at[side, r])
            if r in forward:
                send(piece, piece, self.f_s, self.f_r.at[r], onward)
            self.share(steps, r)

    def opposite(self, r):
        landed(self.piece(2, r), self.f_r.at[r])
        self.share(2, r)

    def prepare(self, steps, turn):
        a, b = (self.x + steps) % 4, (self.yh + turn) % self.turns
        landed(self.buf.at[a * 2 + 1 - self.c, pl.ds(b * 2, 2)], self.c_r.at[steps, turn])
        for q in range(2):
            for k in range(2):
                high, low_part = split(self.buf[a * 2 + q, b * 2 + k])
                block = (a * self.turns + b, pl.ds(k * ROWS, ROWS), pl.ds(q * COLS, COLS))
                self.high[block] = high
                self.low_part[block] = low_part


def kernel(
    s_ref, p_ref, anc, pat, d_ref, oij, ojj,
    pm, sm, sr, sh, sl, pall, ph, pln, pq, pall2, ph2, pln2, cp, zr, cf, cb, xo, lhs, ot, orr, fin, fr,
    y_s, y_r, s_s, s_r, x_s, x_r, f_s, f_r, c_s, c_r, z_s, z_r, b_s, b_r, e_s, e_r, o_s, o_r, h_s, h_r,
    q_s, q_r, y2_s, y2_r, x2_s, x2_r, f2_s, f2_r, c2_s, c2_r,
):
    brow, bcol = lax.axis_index("brow"), lax.axis_index("bcol")
    x, yh, c = brow // 4, brow // 2 % 2, brow % 2
    yl, z = bcol // 8, bcol % 8
    y = yh * 2 + yl
    own = x * 2 + c

    def from_afar(k):
        return jnp.logical_or(bcol // 4 * 4 + yh * 2 + bcol % 2 != brow, k * 8 + x * 2 + c != bcol)


    def at(x, y, z, c):
        return (x * 4 + (y // 2) * 2 + c, (y % 2) * 8 + z)

    def across_y(r):
        return (yh + r // 2) % 2 * 2 + (yl + r % 2) % 2

    def row(a, b, c_steps):
        return (x + a) % 4 * 4 + (yh + b) % 2 * 2 + (c + c_steps) % 2

    def column(a, b):
        return (yl + a) % 2 * 8 + (z + b) % 8

    right, left = at((x + 1) % 4, y, z, c), at((x + 3) % 4, y, z, c)
    up, down = at(x, y, (z + 1) % 8, c), at(x, y, (z + 7) % 8, c)
    sibling = at(x, y, z, 1 - c)
    partner = (brow, (1 - yl) * 8 + z)

    barrier = pltpu.get_barrier_semaphore()

    def greet(device):
        pl.semaphore_signal(barrier, inc=1, device_id=device, device_id_type=MESH)

    for steps in PLANE[1:]:
        greet((row(*steps), bcol))
    for steps in LINE:
        greet((brow, column(*steps)))
    greet(at(x, across_y(3), z, c))
    for k in range(2):
        pl.when(from_afar(k))(lambda k=k: greet((bcol // 4 * 4 + yh * 2 + bcol % 2, k * 8 + x * 2 + c)))

    for half in range(2):
        rows = pl.ds(half * BLOCK, BLOCK)
        pall[own, y, rows, :] = p_ref[yl, rows, :] * anc[yl, 2 * bcol + half].astype(F32)
        pm[rows, :] = p_ref[1 - yl, rows, :] * anc[1 - yl, 2 * bcol + half].astype(F32)

    pl.semaphore_wait(barrier, 31 + sum(jnp.where(from_afar(k), 1, 0) for k in range(2)))

    def to_y(r):
        source = pm if r % 2 else pall.at[own, y]
        send(source, pall.at[own, y], y_s.at[r], y_r.at[r], at(x, across_y(r), z, c))

    devices = (right, left, sibling)
    one = Gather(pall, ph, pln, 2, (x, yh, yl, c), devices, x_s, x_r, f_s, f_r, c_s, c_r)
    two = Gather(pall2, ph2, pln2, 1, (x, yh, yl, c), devices, x2_s, x2_r, f2_s, f2_r, c2_s, c2_r)

    def from_y(r):
        landed(pall.at[own, across_y(r)], y_r.at[r])
        one.spread(r)

    def rows_of(step):
        return pl.ds(pl.multiple_of((z + step) % 8 * PIECE, PIECE), PIECE)

    def scatter():
        for step in range(1, 8):
            device = (brow, yl * 8 + (z + step) % 8)
            send(pall.at[own, y, rows_of(step)], pall2.at[own, yl, rows_of(0)], q_s, q_r.at[0], device)
            send(pm.at[rows_of(step)], pq.at[rows_of(0)], q_s, q_r.at[1], device)
        pall2[own, yl, rows_of(0), :] = pall[own, y, rows_of(0), :]
        pq[rows_of(0), :] = pm[rows_of(0), :]

    def scattered():
        landed(pall2.at[own, yl, pl.ds(0, 7 * PIECE)], q_r.at[0])
        landed(pq.at[pl.ds(0, 7 * PIECE)], q_r.at[1])

    def exchange():
        send(pq, pall2.at[own, yl], y2_s, y2_r, partner)

    def exchanged():
        landed(pall2.at[own, 1 - yl], y2_r)
        two.spread(1)

    def swap(g):
        send(sm.at[g], sr.at[g], s_s.at[g], s_r.at[g], partner)

    to_y(1)
    to_y(3)
    one.spread(0)
    scatter()

    for g in range(GROUPS):
        for p in range(8):
            for k in range(2):
                columns = pl.ds(k * BLOCK, BLOCK)
                sm[g, pl.ds(p * PART, PART), columns] = (
                    s_ref[pl.ds(p * PIECE + g * PART, PART), columns] * pat[p // 4, k].astype(F32)
                )

    def place(g, value, index):
        high, low_part = split(value)
        for k in range(2):
            @pl.when(index == k)
            def _():
                sh[g, :, pl.ds(k * ROWS, ROWS)] = high
                sl[g, :, pl.ds(k * ROWS, ROWS)] = low_part

    def swapped(g):
        landed(sr.at[g], s_r.at[g])
        place(g, sr[g], 1 - yl)

    def multiply(n):
        g, steps, turn = UNITS[n]
        v = (x + steps) % 4 * 2 + (yh + turn) % 2
        a, b, value = sh[g], sl[g], ph[v]
        got = dot(a, pln[v]) + dot(b, value) + dot(a, value)
        cp[n] = got.reshape(8, PART, 2 * COLS)

    rings = [
        Ring(cp.at[n], zr.at[n], z_s.at[n], z_r.at[n], z, (up, down)) for n in range(len(UNITS))
    ]
    keep = -anc[yl, 2 * brow + z // 4].astype(F32)

    def finish(n):
        g, steps, turn = UNITS[n]
        total = rings[n].total() * keep
        for q in range(2):
            j = (x + steps) % 4 * 4 + (yh + turn) % 2 * 2 + q
            cf[j, pl.ds(g * PART, PART), :] = total[:, q * COLS : (q + 1) * COLS]
        if g == GROUPS - 1:
            for a, b, d in PLANE[1:]:
                if a == steps:
                    source, target = cf.at[row(a, turn, d)], cb.at[(yh + turn) % 2, brow]
                    send(source, target, b_s, b_r, (row(a, b, d), bcol))

    def out():
        for a, b in LINE:
            send(cf.at[column(a, b)], xo.at[yl, z], e_s, e_r.at[a], (brow, column(a, b)))

    for g in range(GROUPS):
        place(g, sm[g], yl)
    from_y(1)
    swap(0)
    one.neighbours(0)
    from_y(3)
    one.neighbours(1)
    for time in range(len(UNITS) + 4 * LAG):
        for t in (3, 2, 1):
            if 0 <= time - t * LAG < len(UNITS):
                rings[time - t * LAG].step(t)
        if time == 0:
            swapped(0)
            to_y(2)
        if time == 1:
            scattered()
        if time == 3:
            from_y(2)
            swap(1)
            one.opposite(0)
            one.opposite(1)
        if time == 4:
            one.neighbours(3)
            two.spread(0)
        if time == 5:
            one.neighbours(2)
        if time == 7:
            swapped(1)
            exchange()
        if time == 9:
            two.neighbours(0)
        if time == 11:
            exchanged()
        if time == 12:
            one.opposite(3)
            one.opposite(2)
        if time == 16:
            two.neighbours(1)
        if time == 17:
            two.opposite(0)
        if time == 18:
            two.prepare(0, 0)
        if time == 19:
            two.prepare(3, 0)
        if time == 20:
            two.opposite(1)
            two.prepare(1, 0)
        if time == 21:
            two.prepare(2, 0)
        if time < len(UNITS):
            g, steps, turn = UNITS[time]
            if g == 0:
                one.prepare(steps, turn)
            multiply(time)
            rings[time].step(0)
        if time >= 4 * LAG:
            finish(time - 4 * LAG)
    for turn in range(2):
        cb[(yh + turn) % 2, brow] = cf[row(0, turn, 0)]
    out()
    landed(cb.at[:, pl.ds(0, 15)], b_r)

    for k in range(2):
        for half in range(2):
            high, low_part = split(cb[k, pl.ds(half * 8, 8)].reshape(ROWS, COLS).T)
            lhs[0, pl.ds(k * COLS, COLS), pl.ds(half * ROWS, ROWS)] = high
            lhs[1, pl.ds(k * COLS, COLS), pl.ds(half * ROWS, ROWS)] = low_part

    def unit(v, carry):
        a, b, value = lhs[0], lhs[1], ph2[v]
        got = dot(a, pln2[v]) + dot(b, value) + dot(a, value)
        for k in range(2):
            for q in range(2):
                ot[k, v * 2 + q] = got[k * COLS : (k + 1) * COLS, q * COLS : (q + 1) * COLS]
        return carry

    lax.fori_loop(0, 4, unit, 0)
    last = ReduceScatter(
        lambda d, half: ot.at[half, (z + d) % 8],
        lambda way, half, d: orr.at[way, half, d],
        o_s, o_r, up, down,
    )
    for t in range(4):
        last.step(t)
    xo[yl, z] = cf[bcol]

    def home(h):
        return pltpu.make_async_remote_copy(
            src_ref=fin.at[h], dst_ref=fr.at[yl], send_sem=h_s.at[h], recv_sem=h_r.at[yl],
            device_id=(z // 2 * 4 + yh * 2 + z % 2, x * 4 + h * 2 + c), device_id_type=MESH,
        )

    def away(h):
        return jnp.logical_or(z != x * 2 + c, bcol != x * 4 + h * 2 + c)

    for h in range(2):
        fin[h] = last.total(h)
        pl.when(away(h))(lambda h=h: home(h).start())
    landed(xo.at[yl, pl.ds(0, 7)], e_r.at[0])
    landed(xo.at[1 - yl], e_r.at[1])
    oij[...] = xo[...].reshape(2, ROWS, COLS)

    for h in range(2):
        @pl.when(jnp.logical_not(away(h)))
        def _():
            fr[yl] = fin[h]

    for k in range(2):
        pl.when(from_afar(k))(lambda k=k: landed(fr.at[k], h_r.at[k]))
        ojj[k] = d_ref[k] - fr[k].T

    for h in range(2):
        pl.when(away(h))(lambda h=h: home(h).wait_send())
    for r in (1, 2, 3):
        landed(pm, y_s.at[r])
    for g in range(GROUPS):
        landed(sm.at[g], s_s.at[g])
    landed(pq, y2_s)
    landed(pall.at[pl.ds(0, 2)], x_s)
    landed(pall.at[0], f_s)
    landed(pall.at[pl.ds(0, 4)], c_s)
    landed(pall2.at[pl.ds(0, 2)], x2_s)
    landed(pall2.at[0], f2_s)
    landed(pall2.at[pl.ds(0, 4)], c2_s)
    for n in range(len(UNITS)):
        landed(cp.at[n, pl.ds(0, 7)], z_s.at[n])
    landed(cb.at[:, pl.ds(0, 15)], b_s)
    landed(cf.at[pl.ds(0, 15)], e_s)
    landed(cf.at[pl.ds(0, 14)], q_s)
    landed(ot.at[:, pl.ds(0, 7)], o_s)


def on_device(inverse_block, panels, ancestor_blocks, pattern, diag_inverse):
    vmem, smem = pl.BlockSpec(memory_space=pltpu.VMEM), pl.BlockSpec(memory_space=pltpu.SMEM)
    dma = pltpu.SemaphoreType.DMA
    count = len(UNITS)
    semaphores = [
        (4,), (4,), (GROUPS,), (GROUPS,), (), (2, 4), (), (4,), (), (4, 2), (count,), (count, 2, 4), (), (), (), (2,),
        (), (2, 2, 4), (2,), (2,), (), (2,), (), (), (), (2, 2), (), (2,), (), (4, 1),
    ]
    return pl.pallas_call(
        kernel,
        out_shape=(
            jax.ShapeDtypeStruct((2, ROWS, COLS), F32),
            jax.ShapeDtypeStruct((2, COLS, COLS), F32),
        ),
        in_specs=[vmem, vmem, smem, smem, vmem],
        out_specs=(vmem, vmem),
        scratch_shapes=[
            pltpu.VMEM((ROWS, COLS), F32),
            pltpu.VMEM((GROUPS, TALL, ROWS), F32),
            pltpu.VMEM((GROUPS, TALL, ROWS), F32),
            pltpu.VMEM((GROUPS, TALL, 2 * ROWS), BF16),
            pltpu.VMEM((GROUPS, TALL, 2 * ROWS), BF16),
            pltpu.VMEM((8, 4, ROWS, COLS), F32),
            pltpu.VMEM((8, 2 * ROWS, 2 * COLS), BF16),
            pltpu.VMEM((8, 2 * ROWS, 2 * COLS), BF16),
            pltpu.VMEM((ROWS, COLS), F32),
            pltpu.VMEM((8, 2, ROWS, COLS), F32),
            pltpu.VMEM((4, 2 * ROWS, 2 * COLS), BF16),
            pltpu.VMEM((4, 2 * ROWS, 2 * COLS), BF16),
            pltpu.VMEM((count, 8, PART, 2 * COLS), F32),
            pltpu.VMEM((count, 2, 4, PART, 2 * COLS), F32),
            pltpu.VMEM((16, PIECE, COLS), F32),
            pltpu.VMEM((2, 16, PIECE, COLS), F32),
            pltpu.VMEM((2, 8, PIECE, COLS), F32),
            pltpu.VMEM((2, 2 * COLS, 2 * ROWS), BF16),
            pltpu.VMEM((2, 8, COLS, COLS), F32),
            pltpu.VMEM((2, 2, 4, COLS, COLS), F32),
            pltpu.VMEM((2, COLS, COLS), F32),
            pltpu.VMEM((2, COLS, COLS), F32),
        ]
        + [dma(shape) for shape in semaphores],
        compiler_params=pltpu.CompilerParams(
            collective_id=0, has_side_effects=True, vmem_limit_bytes=56 * 2**20
        ),
        cost_estimate=pl.CostEstimate(flops=8 * 10**9, bytes_accessed=3 * 2**20, transcendentals=0),
        name="selected_inverse",
    )(inverse_block, panels, ancestor_blocks, pattern, diag_inverse)


def solution(mesh):
    return jax.shard_map(
        on_device,
        mesh=mesh,
        in_specs=(
            P("brow", "bcol"),
            P(None, "bcol", "brow"),
            P(),
            P("brow", "bcol"),
            P(None, "brow", "bcol"),
        ),
        out_specs=(P(None, "brow", "bcol"), P(None, "brow", "bcol")),
        check_vma=False,
    )
```

```python
import functools

import jax
import jax.numpy as jnp
from jax import lax
from jax.experimental import pallas as pl
from jax.experimental.pallas import tpu as pltpu
from jax.sharding import PartitionSpec as P

MESH = pl.DeviceIdType.MESH
F32, BF16 = jnp.float32, jnp.bfloat16
BLOCK = 256
ROWS, COLS = 512, 128


def split(value):
    high = value.astype(BF16)
    return high, (value - high.astype(F32)).astype(BF16)


def dot(a, b):
    return jnp.dot(a, b, preferred_element_type=F32)


def landed(ref, sem):
    pltpu.make_async_copy(ref, ref, sem).wait()


def send(src, dst, send_sem, recv_sem, device):
    pltpu.make_async_remote_copy(
        src_ref=src, dst_ref=dst, send_sem=send_sem, recv_sem=recv_sem, device_id=device, device_id_type=MESH
    ).start()


class ReduceScatter:
    def __init__(self, part, slots, send_sem, recv_sem, up, down):
        self.part, self.slots = part, slots
        self.send_sem, self.recv_sem = send_sem, recv_sem
        self.to = (up, down)

    def hop(self, way, half, d):
        first = 4 if half == way else 3
        mine = self.part(d if way == 0 else 8 - d, half)
        if d < first:
            slot = self.slots(way, half, d)
            landed(slot, self.recv_sem.at[way, half, d])
            mine[...] = mine[...] + slot[...]
        send(
            mine,
            self.slots(way, half, d - 1),
            self.send_sem,
            self.recv_sem.at[way, half, d - 1],
            self.to[way],
        )

    def step(self, t):
        for way, half in ((0, 0), (1, 1), (0, 1), (1, 0)):
            first = 4 if half == way else 3
            if first - t >= 1:
                self.hop(way, half, first - t)

    def total(self, half):
        up, down = self.slots(0, half, 0), self.slots(1, half, 0)
        landed(up, self.recv_sem.at[0, half, 0])
        landed(down, self.recv_sem.at[1, half, 0])
        return self.part(0, half)[...] + up[...] + down[...]


GROUPS = 2
PIECE = ROWS // 8
PART = PIECE // GROUPS
TALL = ROWS // GROUPS
LAG = 2
UNITS = [
    (0, 0, 0), (0, 3, 0), (0, 1, 0), (0, 2, 0), (0, 0, 1), (0, 3, 1), (0, 1, 1), (1, 0, 0),
    (1, 3, 0), (1, 1, 0), (1, 2, 0), (1, 0, 1), (0, 2, 1), (1, 3, 1), (1, 1, 1), (1, 2, 1),
]
GROUPS_DONE = [unit[1:] for unit in UNITS if unit[0] == 1]
OUT_TIME = [21, 22]
OUT_LATER = len(OUT_TIME)
PLANE = [(a, b, c) for b in range(2) for a in (0, 3, 1, 2) for c in range(2)]
LINE = [(a, b) for b in range(8) for a in range(2)][1:]


class Ring:
    def __init__(self, terms, slots, send_sem, recv_sem, z, to):
        self.terms, self.slots = terms, slots
        self.send_sem, self.recv_sem, self.z, self.to = send_sem, recv_sem, z, to

    def step(self, t):
        d = 4 - t
        for way in range(2):
            mine = self.terms.at[(self.z + (d if way == 0 else 8 - d)) % 8]
            half = pl.ds(way * (PART // 2), PART // 2)
            target = self.slots.at[way, d - 1]
            if d == 4:
                mine, target = mine.at[half], target.at[half]
            else:
                slot, into = self.slots.at[way, d], mine
                if d == 3:
                    slot, into = slot.at[half], mine.at[half]
                landed(slot, self.recv_sem.at[way, d])
                into[...] = into[...] + slot[...]
            send(mine, target, self.send_sem, self.recv_sem.at[way, d - 1], self.to[way])

    def total(self):
        for way in range(2):
            landed(self.slots.at[way, 0], self.recv_sem.at[way, 0])
        return self.terms[self.z] + self.slots[0, 0] + self.slots[1, 0]


class Gather:
    def __init__(self, buf, high, low_part, turns, place, devices, x_s, x_r, f_s, f_r, c_s, c_r):
        self.buf, self.high, self.low_part, self.turns = buf, high, low_part, turns
        self.x, self.yh, self.yl, self.c = place
        self.right, self.left, self.sibling = devices
        self.x_s, self.x_r, self.f_s, self.f_r, self.c_s, self.c_r = x_s, x_r, f_s, f_r, c_s, c_r

    def piece(self, steps, r, other=0):
        block = (self.yh + r // 2) % self.turns * 2 + (self.yl + r % 2) % 2
        return self.buf.at[(self.x + steps) % 4 * 2 + (self.c + other) % 2, block]

    def spread(self, r):
        piece = self.piece(0, r)
        send(piece, piece, self.x_s, self.x_r.at[0, r], self.right)
        send(piece, piece, self.x_s, self.x_r.at[1, r], self.left)
        self.share(0, r)

    def share(self, steps, r):
        piece = self.piece(steps, r)
        send(piece, piece, self.c_s, self.c_r.at[steps, r // 2], self.sibling)

    def neighbours(self, r):
        for side, steps, onward, forward in ((0, 3, self.right, (0, 3)), (1, 1, self.left, (1, 2))):
            piece = self.piece(steps, r)
            landed(piece, self.x_r.at[side, r])
            if r in forward:
                send(piece, piece, self.f_s, self.f_r.at[r], onward)
            self.share(steps, r)

    def opposite(self, r):
        landed(self.piece(2, r), self.f_r.at[r])
        self.share(2, r)

    def prepare(self, steps, turn):
        a, b = (self.x + steps) % 4, (self.yh + turn) % self.turns
        landed(self.buf.at[a * 2 + 1 - self.c, pl.ds(b * 2, 2)], self.c_r.at[steps, turn])
        for q in range(2):
            for k in range(2):
                high, low_part = split(self.buf[a * 2 + q, b * 2 + k])
                block = (a * self.turns + b, pl.ds(k * ROWS, ROWS), pl.ds(q * COLS, COLS))
                self.high[block] = high
                self.low_part[block] = low_part


def kernel(
    s_hbm, p_hbm, anc, pat, oij, ojj,
    s_ref, p_ref, in_sem,
    pm, sm, sr, sh, sl, pall, ph, pln, pq, pall2, ph2, pln2, cp, zr, cf, cb, xo, lhs, ot, orr, fin, fr,
    y_s, y_r, s_s, s_r, x_s, x_r, f_s, f_r, c_s, c_r, z_s, z_r, b_s, b_r, e_s, e_r, o_s, o_r, h_s, h_r,
    q_s, q_r, y2_s, y2_r, x2_s, x2_r, f2_s, f2_r, c2_s, c2_r,
):
    brow, bcol = lax.axis_index("brow"), lax.axis_index("bcol")
    x, yh, c = brow // 4, brow // 2 % 2, brow % 2
    yl, z = bcol // 8, bcol % 8
    y = yh * 2 + yl
    own = x * 2 + c

    def from_afar(k):
        return jnp.logical_or(bcol // 4 * 4 + yh * 2 + bcol % 2 != brow, k * 8 + x * 2 + c != bcol)


    def at(x, y, z, c):
        return (x * 4 + (y // 2) * 2 + c, (y % 2) * 8 + z)

    def across_y(r):
        return (yh + r // 2) % 2 * 2 + (yl + r % 2) % 2

    def row(a, b, c_steps):
        return (x + a) % 4 * 4 + (yh + b) % 2 * 2 + (c + c_steps) % 2

    def column(a, b):
        return (yl + a) % 2 * 8 + (z + b) % 8

    right, left = at((x + 1) % 4, y, z, c), at((x + 3) % 4, y, z, c)
    up, down = at(x, y, (z + 1) % 8, c), at(x, y, (z + 7) % 8, c)
    sibling = at(x, y, z, 1 - c)
    partner = (brow, (1 - yl) * 8 + z)

    loads = [pltpu.make_async_copy(a, b, in_sem.at[k]) for k, (a, b) in enumerate(((p_hbm, p_ref), (s_hbm, s_ref)))]
    for load in loads:
        load.start()
    barrier = pltpu.get_barrier_semaphore()

    def greet(device):
        pl.semaphore_signal(barrier, inc=1, device_id=device, device_id_type=MESH)

    for steps in PLANE[1:]:
        greet((row(*steps), bcol))
    for steps in LINE:
        greet((brow, column(*steps)))
    greet(at(x, across_y(3), z, c))
    for k in range(2):
        pl.when(from_afar(k))(lambda k=k: greet((bcol // 4 * 4 + yh * 2 + bcol % 2, k * 8 + x * 2 + c)))

    loads[0].wait()
    for half in range(2):
        rows = pl.ds(half * BLOCK, BLOCK)
        pall[own, y, rows, :] = p_ref[yl, rows, :] * anc[yl, 2 * bcol + half].astype(F32)
        pm[rows, :] = p_ref[1 - yl, rows, :] * anc[1 - yl, 2 * bcol + half].astype(F32)

    pl.semaphore_wait(barrier, 31 + sum(jnp.where(from_afar(k), 1, 0) for k in range(2)))

    def to_y(r):
        source = pm if r % 2 else pall.at[own, y]
        send(source, pall.at[own, y], y_s.at[r], y_r.at[r], at(x, across_y(r), z, c))

    devices = (right, left, sibling)
    one = Gather(pall, ph, pln, 2, (x, yh, yl, c), devices, x_s, x_r, f_s, f_r, c_s, c_r)
    two = Gather(pall2, ph2, pln2, 1, (x, yh, yl, c), devices, x2_s, x2_r, f2_s, f2_r, c2_s, c2_r)

    def from_y(r):
        landed(pall.at[own, across_y(r)], y_r.at[r])
        one.spread(r)

    def rows_of(step):
        return pl.ds(pl.multiple_of((z + step) % 8 * PIECE, PIECE), PIECE)

    def scatter():
        for step in range(1, 8):
            device = (brow, yl * 8 + (z + step) % 8)
            send(pall.at[own, y, rows_of(step)], pall2.at[own, yl, rows_of(0)], q_s, q_r.at[0], device)
            send(pm.at[rows_of(step)], pq.at[rows_of(0)], q_s, q_r.at[1], device)
        pall2[own, yl, rows_of(0), :] = pall[own, y, rows_of(0), :]
        pq[rows_of(0), :] = pm[rows_of(0), :]

    def scattered():
        landed(pall2.at[own, yl, pl.ds(0, 7 * PIECE)], q_r.at[0])
        landed(pq.at[pl.ds(0, 7 * PIECE)], q_r.at[1])

    def exchange():
        send(pq, pall2.at[own, yl], y2_s, y2_r, partner)

    def exchanged():
        landed(pall2.at[own, 1 - yl], y2_r)
        two.spread(1)

    def swap(g):
        send(sm.at[g], sr.at[g], s_s.at[g], s_r.at[g], partner)

    to_y(1)
    to_y(3)
    one.spread(0)
    scatter()

    loads[1].wait()
    for g in range(GROUPS):
        for p in range(8):
            for k in range(2):
                columns = pl.ds(k * BLOCK, BLOCK)
                sm[g, pl.ds(p * PART, PART), columns] = (
                    s_ref[pl.ds(p * PIECE + g * PART, PART), columns] * pat[p // 4, k].astype(F32)
                )

    def place(g, value, index):
        high, low_part = split(value)
        for k in range(2):
            @pl.when(index == k)
            def _():
                sh[g, :, pl.ds(k * ROWS, ROWS)] = high
                sl[g, :, pl.ds(k * ROWS, ROWS)] = low_part

    def swapped(g):
        landed(sr.at[g], s_r.at[g])
        place(g, sr[g], 1 - yl)

    def multiply(n):
        g, steps, turn = UNITS[n]
        v = (x + steps) % 4 * 2 + (yh + turn) % 2
        a, b, value = sh[g], sl[g], ph[v]
        got = dot(a, pln[v]) + dot(b, value) + dot(a, value)
        cp[n] = got.reshape(8, PART, 2 * COLS)

    rings = [
        Ring(cp.at[n], zr.at[n], z_s.at[n], z_r.at[n], z, (up, down)) for n in range(len(UNITS))
    ]
    keep = anc[yl, 2 * brow + z // 4].astype(F32)

    def finish(n):
        g, steps, turn = UNITS[n]
        total = rings[n].total() * keep
        for q in range(2):
            j = (x + steps) % 4 * 4 + (yh + turn) % 2 * 2 + q
            cf[j, pl.ds(g * PART, PART), :] = total[:, q * COLS : (q + 1) * COLS]
        if g == GROUPS - 1:
            for a, b, d in PLANE[1:]:
                if a == steps:
                    source, target = cf.at[row(a, turn, d)], cb.at[(yh + turn) % 2, brow]
                    send(source, target, b_s, b_r, (row(a, b, d), bcol))

    def out(steps, turn):
        for k in range(2):
            j = row(steps, turn, k)
            pl.when(j != bcol)(
                lambda j=j: send(cf.at[j], xo.at[yl, z], e_s, e_r.at[(j // 8 + yl) % 2], (brow, j))
            )

    for g in range(GROUPS):
        place(g, sm[g], yl)
    from_y(1)
    swap(0)
    one.neighbours(0)
    from_y(3)
    one.neighbours(1)
    for time in range(len(UNITS) + 4 * LAG):
        for t in (3, 2, 1):
            if 0 <= time - t * LAG < len(UNITS):
                rings[time - t * LAG].step(t)
        if time == 0:
            swapped(0)
            to_y(2)
        if time == 1:
            scattered()
        if time == 3:
            from_y(2)
            swap(1)
            one.opposite(0)
            one.opposite(1)
        if time == 4:
            one.neighbours(3)
            two.spread(0)
        if time == 5:
            one.neighbours(2)
        if time == 7:
            swapped(1)
            exchange()
        if time == 9:
            two.neighbours(0)
        if time == 11:
            exchanged()
        if time == 12:
            one.opposite(3)
            one.opposite(2)
        if time == 16:
            two.neighbours(1)
        if time == 17:
            two.opposite(0)
        if time == 18:
            two.prepare(0, 0)
        if time == 19:
            two.prepare(3, 0)
        if time == 20:
            two.opposite(1)
            two.prepare(1, 0)
        if time == 21:
            two.prepare(2, 0)
        if time < len(UNITS):
            g, steps, turn = UNITS[time]
            if g == 0:
                one.prepare(steps, turn)
            multiply(time)
            rings[time].step(0)
        if time >= 4 * LAG:
            finish(time - 4 * LAG)
        for k in range(OUT_LATER):
            if OUT_TIME[k] == time:
                out(*GROUPS_DONE[k])
    for turn in range(2):
        cb[(yh + turn) % 2, brow] = cf[row(0, turn, 0)]
    for group in GROUPS_DONE[OUT_LATER:]:
        out(*group)
    landed(cb.at[:, pl.ds(0, 15)], b_r)

    for k in range(2):
        for half in range(2):
            high, low_part = split(cb[k, pl.ds(half * 8, 8)].reshape(ROWS, COLS).T)
            lhs[0, pl.ds(k * COLS, COLS), pl.ds(half * ROWS, ROWS)] = high
            lhs[1, pl.ds(k * COLS, COLS), pl.ds(half * ROWS, ROWS)] = low_part

    def unit(v, carry):
        a, b, value = lhs[0], lhs[1], ph2[v]
        got = dot(a, pln2[v]) + dot(b, value) + dot(a, value)
        for k in range(2):
            for q in range(2):
                ot[k, v * 2 + q] = got[k * COLS : (k + 1) * COLS, q * COLS : (q + 1) * COLS]
        return carry

    lax.fori_loop(0, 4, unit, 0)
    last = ReduceScatter(
        lambda d, half: ot.at[half, (z + d) % 8],
        lambda way, half, d: orr.at[way, half, d],
        o_s, o_r, up, down,
    )
    for t in range(4):
        last.step(t)
    xo[yl, z] = cf[bcol]

    def home(h):
        return pltpu.make_async_remote_copy(
            src_ref=fin.at[h], dst_ref=fr.at[yl], send_sem=h_s.at[h], recv_sem=h_r.at[yl],
            device_id=(z // 2 * 4 + yh * 2 + z % 2, x * 4 + h * 2 + c), device_id_type=MESH,
        )

    def away(h):
        return jnp.logical_or(z != x * 2 + c, bcol != x * 4 + h * 2 + c)

    for h in range(2):
        fin[h] = last.total(h)
        pl.when(away(h))(lambda h=h: home(h).start())
    landed(xo.at[yl, pl.ds(0, 7)], e_r.at[0])
    landed(xo.at[1 - yl], e_r.at[1])
    oij[...] = xo[...].reshape(2, ROWS, COLS)

    for h in range(2):
        @pl.when(jnp.logical_not(away(h)))
        def _():
            fr[yl] = fin[h]

    for k in range(2):
        pl.when(from_afar(k))(lambda k=k: landed(fr.at[k], h_r.at[k]))
        ojj[k] = fr[k].T

    for h in range(2):
        pl.when(away(h))(lambda h=h: home(h).wait_send())
    for r in (1, 2, 3):
        landed(pm, y_s.at[r])
    for g in range(GROUPS):
        landed(sm.at[g], s_s.at[g])
    landed(pq, y2_s)
    landed(pall.at[pl.ds(0, 2)], x_s)
    landed(pall.at[0], f_s)
    landed(pall.at[pl.ds(0, 4)], c_s)
    landed(pall2.at[pl.ds(0, 2)], x2_s)
    landed(pall2.at[0], f2_s)
    landed(pall2.at[pl.ds(0, 4)], c2_s)
    for n in range(len(UNITS)):
        landed(cp.at[n, pl.ds(0, 7)], z_s.at[n])
    landed(cb.at[:, pl.ds(0, 15)], b_s)
    landed(cf.at[pl.ds(0, 15)], e_s)
    landed(cf.at[pl.ds(0, 14)], q_s)
    landed(ot.at[:, pl.ds(0, 7)], o_s)


def on_device(inverse_block, panels, ancestor_blocks, pattern, diag_inverse):
    vmem, smem = pl.BlockSpec(memory_space=pltpu.VMEM), pl.BlockSpec(memory_space=pltpu.SMEM)
    hbm = pl.BlockSpec(memory_space=pl.ANY)
    dma = pltpu.SemaphoreType.DMA
    count = len(UNITS)
    semaphores = [
        (4,), (4,), (GROUPS,), (GROUPS,), (), (2, 4), (), (4,), (), (4, 2), (count,), (count, 2, 4), (), (), (), (2,),
        (), (2, 2, 4), (2,), (2,), (), (2,), (), (), (), (2, 2), (), (2,), (), (4, 1),
    ]
    product, diagonal = pl.pallas_call(
        kernel,
        out_shape=(
            jax.ShapeDtypeStruct((2, ROWS, COLS), F32),
            jax.ShapeDtypeStruct((2, COLS, COLS), F32),
        ),
        in_specs=[hbm, hbm, smem, smem],
        out_specs=(vmem, vmem),
        scratch_shapes=[
            pltpu.VMEM((ROWS, ROWS), F32),
            pltpu.VMEM((2, ROWS, COLS), F32),
            dma((2,)),
            pltpu.VMEM((ROWS, COLS), F32),
            pltpu.VMEM((GROUPS, TALL, ROWS), F32),
            pltpu.VMEM((GROUPS, TALL, ROWS), F32),
            pltpu.VMEM((GROUPS, TALL, 2 * ROWS), BF16),
            pltpu.VMEM((GROUPS, TALL, 2 * ROWS), BF16),
            pltpu.VMEM((8, 4, ROWS, COLS), F32),
            pltpu.VMEM((8, 2 * ROWS, 2 * COLS), BF16),
            pltpu.VMEM((8, 2 * ROWS, 2 * COLS), BF16),
            pltpu.VMEM((ROWS, COLS), F32),
            pltpu.VMEM((8, 2, ROWS, COLS), F32),
            pltpu.VMEM((4, 2 * ROWS, 2 * COLS), BF16),
            pltpu.VMEM((4, 2 * ROWS, 2 * COLS), BF16),
            pltpu.VMEM((count, 8, PART, 2 * COLS), F32),
            pltpu.VMEM((count, 2, 4, PART, 2 * COLS), F32),
            pltpu.VMEM((16, PIECE, COLS), F32),
            pltpu.VMEM((2, 16, PIECE, COLS), F32),
            pltpu.VMEM((2, 8, PIECE, COLS), F32),
            pltpu.VMEM((2, 2 * COLS, 2 * ROWS), BF16),
            pltpu.VMEM((2, 8, COLS, COLS), F32),
            pltpu.VMEM((2, 2, 4, COLS, COLS), F32),
            pltpu.VMEM((2, COLS, COLS), F32),
            pltpu.VMEM((2, COLS, COLS), F32),
        ]
        + [dma(shape) for shape in semaphores],
        compiler_params=pltpu.CompilerParams(
            collective_id=0, has_side_effects=True, vmem_limit_bytes=56 * 2**20
        ),
        cost_estimate=pl.CostEstimate(flops=8 * 10**9, bytes_accessed=3 * 2**20, transcendentals=0),
        name="selected_inverse",
    )(inverse_block, panels, ancestor_blocks, pattern)
    return -product, diag_inverse + diagonal


def solution(mesh):
    return jax.shard_map(
        on_device,
        mesh=mesh,
        in_specs=(
            P("brow", "bcol"),
            P(None, "bcol", "brow"),
            P(),
            P("brow", "bcol"),
            P(None, "brow", "bcol"),
        ),
        out_specs=(P(None, "brow", "bcol"), P(None, "brow", "bcol")),
        check_vma=False,
    )
```
